32 devices in a mesh: dp: 4 (over x, core), expert: 8 (over z, y).
Axes of the slice: x: 2, y: 2, z: 4, core: 2. Of those that a mesh axis runs over, the one named last changes fastest.
Arguments:
- embeds: bfloat16 [8192, 1152], P(('dp', 'expert')), may hold values from -6 to 6
- trunk_gain: float32 [1152], replicated, may hold values from 0.5 to 1.5
- trunk_weight: bfloat16 [1152, 1152], replicated, may hold values from -0.1875 to 0.1875
- w_gate: bfloat16 [32, 1152, 1024], P(('dp', 'expert')), may hold values from -0.1875 to 0.1875
- w_up: bfloat16 [32, 1152, 1024], P(('dp', 'expert')), may hold values from -0.1875 to 0.1875
- w_down: bfloat16 [32, 1024, 1152], P(('dp', 'expert')), may hold values from -0.1875 to 0.1875
- tags: int32 [8192], P(('dp', 'expert')), may hold values from 0 to 31, as said below
- plan: int32 [32], replicated, may hold values from 0 to 31, as said below
- helper: int32 [8192], P(('dp', 'expert')), may hold values from 0 to 31, as said below
- cotangent: bfloat16 [8192, 1152], P(('dp', 'expert')), may hold values from -0.59765625 to 0.59765625
Outputs:
- grad_gate: bfloat16 [32, 1152, 1024], P(('dp', 'expert'))
- grad_up: bfloat16 [32, 1152, 1024], P(('dp', 'expert'))
- grad_down: bfloat16 [32, 1024, 1152], P(('dp', 'expert'))
- grad_trunk: float32 [1152, 1152], P(('dp', 'expert'))
The draws below stay inside these ranges and needn't reach their ends.
Inputs may be any that keep to these rules, and one draw needn't show every extreme that they name: Each token's helper equals its tag, except for tokens tagged with the expert plan[0], which may go to any device. Each device sends exactly 8 tokens to every device (numbered in the order dp then expert). Every device other than device plan[0] receives exactly 8 tokens tagged plan[0]; device plan[0] receives only tokens tagged plan[0]. `tags`: see helper. A permutation of the 32 experts; only plan[0] is served by helpers.
All inputs are finite; a program needn't handle non-finite values.
Results may differ from the reference program's by a relative error of at most 0.003.
The reference program's roundings to bfloat16 on the way count: a program that leaves them out, or rounds other values in their place, can miss the bound.
Values may be sent and summed in bfloat16 or wider, within the bound.
A program may use at most 128 MiB of HBM per device.

```python
import jax
import jax.numpy as jnp
from jax import lax

D = 1152
FF = 1024
TOK_DEV = 256
EXPERTS = 32
TOKENS = 8192
HOT_CAP = 8


def routing_tables(key):
    capacity = TOK_DEV // EXPERTS
    order = jax.random.permutation(jax.random.fold_in(key, 7), EXPERTS).astype(jnp.int32)
    hot_expert = order[0]
    first_keys = jax.random.split(jax.random.fold_in(key, 11), EXPERTS)
    position = jax.vmap(lambda k: jax.random.permutation(k, TOK_DEV))(first_keys).astype(jnp.int32)
    target = position // capacity
    within = position % capacity
    incoming = jnp.arange(EXPERTS, dtype=jnp.int32)[:, None] * capacity + within
    second_keys = jax.random.split(jax.random.fold_in(key, 13), EXPERTS)
    ranking = jax.vmap(lambda k: jax.random.permutation(k, TOK_DEV))(second_keys).astype(jnp.int32)
    chosen = (ranking[target, incoming] < HOT_CAP) & (target != hot_expert)
    tag_table = jnp.where(chosen, hot_expert, target)
    return (tag_table.reshape(-1).astype(jnp.int32), order, target.reshape(-1).astype(jnp.int32))


def draw_tags(key, part):
    return routing_tables(key)[0]


def draw_plan(key, part):
    return routing_tables(key)[1]


def draw_helper(key, part):
    return routing_tables(key)[2]


def shard_levels(own_key, shape, cuts, least, largest):
    loudness = 1.0
    for dim, shards_of in cuts:
        heights = jax.random.uniform(jax.random.fold_in(jax.random.fold_in(own_key, 6), dim), (shards_of,), jnp.float32, least / len(cuts), largest / len(cuts))
        loudness = loudness * jnp.repeat(jnp.exp(heights), shape[dim] // shards_of).reshape((-1,) + (1,) * (len(shape) - 1 - dim))
    return loudness


def bell_draw(key, dims, width, bound, pieces=(), held_as=jnp.bfloat16):
    values = width * jax.random.normal(key, dims, jnp.float32)
    if pieces:
        values = values * shard_levels(key, dims, pieces, -0.22, 0.18)
    return jnp.clip(values, -bound, bound).astype(held_as)


def setup_inputs(seed: int = 0) -> dict:
    splits = jax.random.split(jax.random.key(seed), 11)
    embeds = bell_draw(splits[0], (TOKENS, D), 1.0, 6.0, ((0, 32),))
    trunk_gain = jnp.clip(1.0 + 0.1 * jax.random.normal(splits[1], (D,), jnp.float32), 0.5, 1.5)
    trunk_weight = bell_draw(splits[2], (D, D), D ** -0.5, 0.1875)
    w_gate = bell_draw(splits[3], (EXPERTS, D, FF), D ** -0.5, 0.1875, ((0, 32),))
    w_up = bell_draw(splits[4], (EXPERTS, D, FF), D ** -0.5, 0.1875, ((0, 32),))
    w_down = bell_draw(splits[5], (EXPERTS, FF, D), FF ** -0.5, 0.1875, ((0, 32),))
    tags = draw_tags(jax.random.fold_in(splits[10], 71), 0)
    plan = draw_plan(jax.random.fold_in(splits[10], 71), 0)
    helper = draw_helper(jax.random.fold_in(splits[10], 71), 0)
    cotangent = bell_draw(splits[9], (TOKENS, D), 0.1, 0.59765625, ((0, 32),))
    return {"embeds": embeds, "trunk_gain": trunk_gain, "trunk_weight": trunk_weight, "w_gate": w_gate, "w_up": w_up, "w_down": w_down, "tags": tags, "plan": plan, "helper": helper, "cotangent": cotangent}


def expert_pass(rows, cotan, gate_w, up_w, down_w):
    gate_pre = jnp.dot(rows, gate_w, preferred_element_type=jnp.float32)
    up_pre = jnp.dot(rows, up_w, preferred_element_type=jnp.float32)
    sigma = jax.nn.sigmoid(gate_pre)
    silu_val = gate_pre * sigma
    active = (silu_val * up_pre).astype(jnp.bfloat16)
    d_active = jnp.dot(cotan, down_w.T, preferred_element_type=jnp.float32)
    d_gate = (d_active * up_pre * sigma * (1.0 + gate_pre * (1.0 - sigma))).astype(jnp.bfloat16)
    d_up = (d_active * silu_val).astype(jnp.bfloat16)
    sum_gate = jnp.dot(rows.T, d_gate, preferred_element_type=jnp.float32)
    sum_up = jnp.dot(rows.T, d_up, preferred_element_type=jnp.float32)
    sum_down = jnp.dot(active.T, cotan, preferred_element_type=jnp.float32)
    d_rows = jnp.dot(d_gate, gate_w.T, preferred_element_type=jnp.float32) + jnp.dot(d_up, up_w.T, preferred_element_type=jnp.float32)
    return (sum_gate, sum_up, sum_down, d_rows)

def reference(embeds, trunk_gain, trunk_weight, w_gate, w_up, w_down, tags, plan, helper, cotangent):
    values = embeds.astype(jnp.float32)
    factor = lax.rsqrt(lax.optimization_barrier(jnp.mean(values * values, axis=1, keepdims=True)) + 1e-06)
    normed = (values * factor * trunk_gain).astype(jnp.bfloat16)
    hidden = (values + jnp.dot(normed, trunk_weight, preferred_element_type=jnp.float32)).astype(jnp.bfloat16)
    hot_expert = plan[0]
    by_device = jnp.argsort(helper, stable=True).astype(jnp.int32).reshape(EXPERTS, TOK_DEV)
    foreign = ((tags == hot_expert) & (helper != hot_expert)).astype(jnp.int32)
    hot_index = jnp.argsort(1 - foreign, stable=True).astype(jnp.int32)[:(EXPERTS - 1) * HOT_CAP]
    hot_gate, hot_up, hot_down, hot_drows = expert_pass(hidden[hot_index], cotangent[hot_index], w_gate[hot_expert], w_up[hot_expert], w_down[hot_expert])

    def one_expert(which):
        index = by_device[which]
        rows = hidden[index]
        owned = tags[index] == which
        cotan = jnp.where(owned[:, None], cotangent[index], jnp.zeros_like(cotangent[index]))
        sum_gate, sum_up, sum_down, d_rows = expert_pass(rows, cotan, w_gate[which], w_up[which], w_down[which])
        is_hot = which == hot_expert
        sum_gate = jnp.where(is_hot, sum_gate + hot_gate, sum_gate).astype(jnp.bfloat16)
        sum_up = jnp.where(is_hot, sum_up + hot_up, sum_up).astype(jnp.bfloat16)
        sum_down = jnp.where(is_hot, sum_down + hot_down, sum_down).astype(jnp.bfloat16)
        return (sum_gate, sum_up, sum_down, d_rows)
    grad_gate, grad_up, grad_down, drow_blocks = lax.map(one_expert, jnp.arange(EXPERTS, dtype=jnp.int32))
    dhidden = jnp.zeros((TOKENS, D), jnp.float32)
    dhidden = dhidden.at[by_device.reshape(-1)].add(drow_blocks.reshape(TOKENS, D))
    dhidden = dhidden.at[hot_index].add(hot_drows).astype(jnp.bfloat16)
    grad_trunk = jnp.dot(normed.T, dhidden, preferred_element_type=jnp.float32)
    return (grad_gate, grad_up, grad_down, grad_trunk)
```

```python
import functools

import jax
import jax.numpy as jnp
from jax import lax
from jax.experimental import pallas as pl
from jax.experimental.pallas import tpu as pltpu
from jax.sharding import PartitionSpec as P

LANES = 128
TILE = 16
MESH = pl.DeviceIdType.MESH


def padded(value, multiple):
    return -(-value // multiple) * multiple


def flat_index(experts_axis):
    return lax.axis_index("dp") * experts_axis + lax.axis_index("expert")


def place(flat, experts_axis):
    return (flat // experts_axis, flat % experts_axis)


def flipped(me, bit):
    weight = 1 << bit
    return me + (1 - 2 * ((me // weight) % 2)) * weight


def greet_all(n, experts_axis):
    me = flat_index(experts_axis)
    barrier = pltpu.get_barrier_semaphore()

    def greet(step, carry):
        pl.semaphore_signal(
            barrier,
            inc=1,
            device_id=place(lax.rem(me + step, n), experts_axis),
            device_id_type=MESH,
        )
        return carry

    lax.fori_loop(1, n, greet, 0)
    pl.semaphore_wait(barrier, n - 1)


def greet_bits(bits, experts_axis):
    me = flat_index(experts_axis)
    barrier = pltpu.get_barrier_semaphore()
    for bit in range(bits):
        pl.semaphore_signal(
            barrier, inc=1, device_id=place(flipped(me, bit), experts_axis), device_id_type=MESH
        )
    pl.semaphore_wait(barrier, bits)


def exchange_kernel(n, experts_axis, send_ref, out_ref, send_sem, recv_sem, own_sem):
    me = flat_index(experts_axis)
    greet_all(n, experts_axis)
    own = pltpu.make_async_copy(send_ref.at[me], out_ref.at[me], own_sem)
    own.start()

    def copy_to(step):
        to = lax.rem(me + step, n)
        return pltpu.make_async_remote_copy(
            src_ref=send_ref.at[to],
            dst_ref=out_ref.at[me],
            send_sem=send_sem.at[to],
            recv_sem=recv_sem.at[me],
            device_id=place(to, experts_axis),
            device_id_type=MESH,
        )

    def copy_from(step):
        source = lax.rem(me + step, n)
        return pltpu.make_async_remote_copy(
            src_ref=send_ref.at[source],
            dst_ref=out_ref.at[source],
            send_sem=send_sem.at[source],
            recv_sem=recv_sem.at[source],
            device_id=place(source, experts_axis),
            device_id_type=MESH,
        )

    def start(step, carry):
        copy_to(step).start()
        return carry

    def finish(step, carry):
        copy = copy_from(step)
        copy.wait_send()
        copy.wait_recv()
        return carry

    lax.fori_loop(1, n, start, 0)
    own.wait()
    lax.fori_loop(1, n, finish, 0)


def exchange(send, n, experts_axis):
    return pl.pallas_call(
        functools.partial(exchange_kernel, n, experts_axis),
        out_shape=jax.ShapeDtypeStruct(send.shape, send.dtype),
        in_specs=[pl.BlockSpec(memory_space=pltpu.VMEM)],
        out_specs=pl.BlockSpec(memory_space=pltpu.VMEM),
        scratch_shapes=[
            pltpu.SemaphoreType.DMA((n,)),
            pltpu.SemaphoreType.DMA((n,)),
            pltpu.SemaphoreType.DMA,
        ],
        compiler_params=pltpu.CompilerParams(
            collective_id=0, has_side_effects=True, vmem_limit_bytes=40 * 1024 * 1024
        ),
    )(send)


def axis_orders(n, experts_axis):
    bits = n.bit_length() - 1
    core = experts_axis.bit_length() - 1
    others = [b for b in range(bits) if b != core]
    low = others[0]
    high = others[-1]
    middle = others[1:-1]
    return core, [
        [high, low] + middle,
        [low] + middle + [high],
        middle + [high, low],
    ]


def column_groups(width):
    tiles = width // LANES
    cuts = [(tiles * g) // 3 * LANES for g in range(4)]
    return [(cuts[g], cuts[g + 1] - cuts[g]) for g in range(3)]


def gather_kernel(n, experts_axis, width, mine_ref, out_ref, *scratch):
    bits = n.bit_length() - 1
    me = flat_index(experts_axis)
    core, orders = axis_orders(n, experts_axis)
    held, send_sem, recv_sem = scratch[:3], scratch[3], scratch[4]
    for group, (first, wide) in enumerate(column_groups(width)):
        held[group][0] = mine_ref[:, first : first + wide]
    greet_bits(bits, experts_axis)
    plans = [order[::-1] + [core] for order in orders]
    for stage in range(bits):
        count = 1 << stage
        copies = []
        for group in range(3):
            bit = plans[group][stage]
            copy = pltpu.make_async_remote_copy(
                src_ref=held[group].at[pl.ds(0, count)],
                dst_ref=held[group].at[pl.ds(count, count)],
                send_sem=send_sem.at[stage, group],
                recv_sem=recv_sem.at[stage, group],
                device_id=place(flipped(me, bit), experts_axis),
                device_id_type=MESH,
            )
            copy.start()
            copies.append(copy)
        for copy in copies:
            copy.wait()
    for group, (first, wide) in enumerate(column_groups(width)):
        for slot in range(n):
            offset = sum(
                1 << plans[group][stage] for stage in range(bits) if (slot >> stage) & 1
            )
            out_ref[offset, :, first : first + wide] = held[group][slot]


def gather(mine, n, experts_axis):
    rows, width = mine.shape
    bits = n.bit_length() - 1
    return pl.pallas_call(
        functools.partial(gather_kernel, n, experts_axis, width),
        out_shape=jax.ShapeDtypeStruct((n, rows, width), mine.dtype),
        in_specs=[pl.BlockSpec(memory_space=pltpu.VMEM)],
        out_specs=pl.BlockSpec(memory_space=pltpu.VMEM),
        scratch_shapes=[
            pltpu.VMEM((n, rows, wide), mine.dtype) for _, wide in column_groups(width)
        ]
        + [pltpu.SemaphoreType.DMA((bits, 3)), pltpu.SemaphoreType.DMA((bits, 3))],
        compiler_params=pltpu.CompilerParams(
            collective_id=1, has_side_effects=True, vmem_limit_bytes=48 * 1024 * 1024
        ),
    )(mine)


def stage_types(bits):
    return [jnp.bfloat16 if stage < 3 else jnp.float32 for stage in range(bits)]


def reduce_kernel(n, experts_axis, block, width, part_ref, out_ref, *scratch):
    bits = n.bit_length() - 1
    me = flat_index(experts_axis)
    core, orders = axis_orders(n, experts_axis)
    plans = [[core] + order for order in orders]
    groups = column_groups(width)
    types = stage_types(bits)
    sums = [[scratch[3 * (s * 3 + g)] for g in range(3)] for s in range(bits)]
    sent = [[scratch[3 * (s * 3 + g) + 1] for g in range(3)] for s in range(bits)]
    came = [[scratch[3 * (s * 3 + g) + 2] for g in range(3)] for s in range(bits)]
    send_sem, recv_sem = scratch[9 * bits], scratch[9 * bits + 1]
    greet_bits(bits, experts_axis)
    left = [sorted(range(bits), reverse=True) for _ in groups]
    for stage in range(bits):
        half = n >> (stage + 1)
        copies = []
        for group, (first, wide) in enumerate(groups):
            bit = plans[group][stage]
            low = 1 << (len(left[group]) - left[group].index(bit) - 1)
            mine = (me // (1 << bit)) % 2

            def read(item, side, low=low, stage=stage, group=group, first=first, wide=wide):
                at = (item // low) * (2 * low) + side * low + item % low
                if stage == 0:
                    return part_ref[at, :, first : first + wide]
                return sums[stage - 1][group][at]

            def pack(item, carry, read=read, mine=mine, stage=stage, group=group):
                sent[stage][group][item] = read(item, 1 - mine).astype(types[stage])
                return carry

            lax.fori_loop(0, half, pack, 0)
            copy = pltpu.make_async_remote_copy(
                src_ref=sent[stage][group],
                dst_ref=came[stage][group],
                send_sem=send_sem.at[stage, group],
                recv_sem=recv_sem.at[stage, group],
                device_id=place(flipped(me, bit), experts_axis),
                device_id_type=MESH,
            )
            copy.start()
            copies.append((copy, read, mine))
            left[group].remove(bit)
        for group in range(3):
            copy, read, mine = copies[group]
            copy.wait()

            def add(item, carry, read=read, mine=mine, stage=stage, group=group):
                sums[stage][group][item] = read(item, mine) + came[stage][group][item].astype(
                    jnp.float32
                )
                return carry

            lax.fori_loop(0, half, add, 0)
    for group, (first, wide) in enumerate(groups):
        out_ref[:, first : first + wide] = sums[bits - 1][group][0]


def reduce_scatter(part, n, experts_axis):
    block, width = part.shape[1:]
    bits = n.bit_length() - 1
    types = stage_types(bits)
    scratch = []
    for stage in range(bits):
        half = n >> (stage + 1)
        for _, wide in column_groups(width):
            scratch.append(pltpu.VMEM((half, block, wide), jnp.float32))
            scratch.append(pltpu.VMEM((half, block, wide), types[stage]))
            scratch.append(pltpu.VMEM((half, block, wide), types[stage]))
    return pl.pallas_call(
        functools.partial(reduce_kernel, n, experts_axis, block, width),
        out_shape=jax.ShapeDtypeStruct((block, width), jnp.float32),
        in_specs=[pl.BlockSpec(memory_space=pltpu.VMEM)],
        out_specs=pl.BlockSpec(memory_space=pltpu.VMEM),
        scratch_shapes=scratch
        + [pltpu.SemaphoreType.DMA((bits, 3)), pltpu.SemaphoreType.DMA((bits, 3))],
        compiler_params=pltpu.CompilerParams(
            collective_id=2, has_side_effects=True, vmem_limit_bytes=52 * 1024 * 1024
        ),
    )(part)


def lines_of(blocks, count, rows, first):
    lines = blocks.shape[0]
    wanted = jnp.arange(lines // rows * count, dtype=jnp.int32)
    wanted = wanted // count * rows + first + wanted % count
    chosen = wanted[:, None] == jnp.arange(lines, dtype=jnp.int32)[None, :]
    return jnp.dot(
        chosen.astype(jnp.bfloat16), blocks, preferred_element_type=jnp.float32
    ).astype(jnp.bfloat16)


def trunk(rows, gain, weight):
    values = rows.astype(jnp.float32)
    factor = lax.rsqrt(jnp.mean(values * values, axis=1, keepdims=True) + 1e-06)
    normed = (values * factor * gain).astype(jnp.bfloat16)
    hidden = values + jnp.dot(normed, weight, preferred_element_type=jnp.float32)
    return normed, hidden.astype(jnp.bfloat16)


def dot_t(a, b):
    return lax.dot_general(a, b, (((1,), (1,)), ((), ())), preferred_element_type=jnp.float32)


def t_dot(a, b):
    return lax.dot_general(a, b, (((0,), (0,)), ((), ())), preferred_element_type=jnp.float32)


def through_expert(hidden, cotan, gate_w, up_w, down_w):
    gate_pre = jnp.dot(hidden, gate_w, preferred_element_type=jnp.float32)
    up_pre = jnp.dot(hidden, up_w, preferred_element_type=jnp.float32)
    sigma = jax.nn.sigmoid(gate_pre)
    silu_val = gate_pre * sigma
    active = (silu_val * up_pre).astype(jnp.bfloat16)
    d_active = dot_t(cotan, down_w)
    d_gate = (d_active * up_pre * sigma * (1.0 + gate_pre * (1.0 - sigma))).astype(jnp.bfloat16)
    d_up = (d_active * silu_val).astype(jnp.bfloat16)
    d_rows = (dot_t(d_gate, gate_w) + dot_t(d_up, up_w)).astype(jnp.bfloat16)
    return active, d_gate, d_up, d_rows


def body(embeds, trunk_gain, trunk_weight, w_gate, w_up, w_down, tags, plan, helper, cotangent):
    n = lax.axis_size(("dp", "expert"))
    experts_axis = lax.axis_size("expert")
    device = flat_index(experts_axis)
    hot_expert = plan[0]
    tokens, feature = embeds.shape
    capacity = tokens // n
    hot_slots = tokens // 32
    rows = padded(2 * capacity, TILE)
    gate_w, up_w, down_w = w_gate[0], w_up[0], w_down[0]

    token = jnp.arange(tokens, dtype=jnp.int32)
    before = (helper[:, None] == helper[None, :]) & (token[:, None] > token[None, :])
    slot = jnp.sum(before.astype(jnp.int32), axis=1)
    target = helper * rows + slot
    line = jnp.arange(n * rows, dtype=jnp.int32)
    pick = jnp.concatenate(
        [line[:, None] == target[None, :], line[:, None] == target[None, :] + capacity], axis=1
    ).astype(jnp.bfloat16)
    flagged = ((tags == hot_expert) & (helper != hot_expert)).astype(jnp.bfloat16)
    flag_lanes = jnp.broadcast_to(flagged[:, None], (tokens, LANES))
    content = jnp.concatenate(
        [
            jnp.concatenate([embeds, flag_lanes], axis=1),
            jnp.concatenate([cotangent, jnp.zeros_like(flag_lanes)], axis=1),
        ],
        axis=0,
    )
    send = jnp.dot(pick, content, preferred_element_type=jnp.float32).astype(jnp.bfloat16)
    got = exchange(send.reshape(n, rows, feature + LANES), n, experts_axis)
    got = got.reshape(n * rows, feature + LANES)
    got_wide = lines_of(got, capacity, rows, 0)
    got_embeds = got_wide[:, :feature]
    got_cotan = lines_of(got[:, :feature], capacity, rows, capacity)
    flags = got_wide[:, feature] > 0

    rank = jnp.sum((flags[None, :] & (token[:, None] > token[None, :])).astype(jnp.int32), axis=1)
    picker = (rank[None, :] == jnp.arange(hot_slots, dtype=jnp.int32)[:, None]) & flags[None, :]
    picker = picker.astype(jnp.bfloat16)
    hot = jnp.concatenate(
        [
            jnp.dot(picker, got_embeds, preferred_element_type=jnp.float32),
            jnp.dot(picker, got_cotan, preferred_element_type=jnp.float32),
        ],
        axis=0,
    ).astype(jnp.bfloat16)
    pooled = gather(hot, n, experts_axis)
    pooled = pooled.reshape(n * 2 * hot_slots, feature)
    hot_embeds = lines_of(pooled, hot_slots, 2 * hot_slots, 0)
    hot_cotan = lines_of(pooled, hot_slots, 2 * hot_slots, hot_slots)
    is_owner = device == hot_expert
    hot_cotan = jnp.where(is_owner, hot_cotan, jnp.zeros_like(hot_cotan))
    own_cotan = jnp.where(flags[:, None], jnp.zeros_like(got_cotan), got_cotan)

    all_embeds = jnp.concatenate([got_embeds, hot_embeds], axis=0)
    all_cotan = jnp.concatenate([own_cotan, hot_cotan], axis=0)
    normed, hidden = trunk(all_embeds, trunk_gain, trunk_weight)
    active, d_gate, d_up, d_rows = through_expert(hidden, all_cotan, gate_w, up_w, down_w)

    share = feature // n
    block = padded(share, TILE)
    spread = jnp.pad(
        normed.reshape(normed.shape[0], n, share), ((0, 0), (0, 0), (0, block - share))
    ).reshape(normed.shape[0], n * block)
    part = t_dot(spread, d_rows).reshape(n, block, feature)
    grad_trunk = reduce_scatter(part, n, experts_axis)[:share]

    grad_gate = t_dot(hidden, d_gate).astype(jnp.bfloat16)[None]
    grad_up = t_dot(hidden, d_up).astype(jnp.bfloat16)[None]
    grad_down = t_dot(active, all_cotan).astype(jnp.bfloat16)[None]
    return (grad_gate, grad_up, grad_down, grad_trunk)


def solution(mesh):
    spread_rows = P(("dp", "expert"), None)
    spread_first = P(("dp", "expert"), None, None)
    return jax.shard_map(
        body,
        mesh=mesh,
        in_specs=(
            spread_rows,
            P(),
            P(),
            spread_first,
            spread_first,
            spread_first,
            P(("dp", "expert")),
            P(),
            P(("dp", "expert")),
            spread_rows,
        ),
        out_specs=(spread_first, spread_first, spread_first, spread_rows),
        check_vma=False,
    )
```

```python
import functools

import jax
import jax.numpy as jnp
from jax import lax
from jax.experimental import pallas as pl
from jax.experimental.pallas import tpu as pltpu
from jax.sharding import PartitionSpec as P

LANES = 128
TILE = 16
MESH = pl.DeviceIdType.MESH


def padded(value, multiple):
    return -(-value // multiple) * multiple


def flat_index(experts_axis):
    return lax.axis_index("dp") * experts_axis + lax.axis_index("expert")


def place(flat, experts_axis):
    return (flat // experts_axis, flat % experts_axis)


def flipped(me, bit):
    weight = 1 << bit
    return me + (1 - 2 * ((me // weight) % 2)) * weight


def greet_all(n, experts_axis):
    me = flat_index(experts_axis)
    barrier = pltpu.get_barrier_semaphore()

    def greet(step, carry):
        pl.semaphore_signal(
            barrier,
            inc=1,
            device_id=place(lax.rem(me + step, n), experts_axis),
            device_id_type=MESH,
        )
        return carry

    lax.fori_loop(1, n, greet, 0)
    pl.semaphore_wait(barrier, n - 1)


def greet_bits(bits, experts_axis):
    me = flat_index(experts_axis)
    barrier = pltpu.get_barrier_semaphore()
    for bit in range(bits):
        pl.semaphore_signal(
            barrier, inc=1, device_id=place(flipped(me, bit), experts_axis), device_id_type=MESH
        )
    pl.semaphore_wait(barrier, bits)


def exchange_kernel(n, experts_axis, send_ref, out_ref, send_sem, recv_sem, own_sem):
    me = flat_index(experts_axis)
    greet_all(n, experts_axis)
    own = pltpu.make_async_copy(send_ref.at[me], out_ref.at[me], own_sem)
    own.start()

    def copy_to(step):
        to = lax.rem(me + step, n)
        return pltpu.make_async_remote_copy(
            src_ref=send_ref.at[to],
            dst_ref=out_ref.at[me],
            send_sem=send_sem.at[to],
            recv_sem=recv_sem.at[me],
            device_id=place(to, experts_axis),
            device_id_type=MESH,
        )

    def copy_from(step):
        source = lax.rem(me + step, n)
        return pltpu.make_async_remote_copy(
            src_ref=send_ref.at[source],
            dst_ref=out_ref.at[source],
            send_sem=send_sem.at[source],
            recv_sem=recv_sem.at[source],
            device_id=place(source, experts_axis),
            device_id_type=MESH,
        )

    def start(step, carry):
        copy_to(step).start()
        return carry

    def finish(step, carry):
        copy = copy_from(step)
        copy.wait_send()
        copy.wait_recv()
        return carry

    lax.fori_loop(1, n, start, 0)
    own.wait()
    lax.fori_loop(1, n, finish, 0)


def exchange(send, n, experts_axis):
    return pl.pallas_call(
        functools.partial(exchange_kernel, n, experts_axis),
        out_shape=jax.ShapeDtypeStruct(send.shape, send.dtype),
        in_specs=[pl.BlockSpec(memory_space=pltpu.VMEM)],
        out_specs=pl.BlockSpec(memory_space=pltpu.VMEM),
        scratch_shapes=[
            pltpu.SemaphoreType.DMA((n,)),
            pltpu.SemaphoreType.DMA((n,)),
            pltpu.SemaphoreType.DMA,
        ],
        compiler_params=pltpu.CompilerParams(
            collective_id=0, has_side_effects=True, vmem_limit_bytes=40 * 1024 * 1024
        ),
    )(send)


def axis_orders(n, experts_axis):
    bits = n.bit_length() - 1
    core = experts_axis.bit_length() - 1
    others = [b for b in range(bits) if b != core]
    low = others[0]
    high = others[-1]
    middle = others[1:-1]
    return core, [
        [high, low] + middle,
        [low] + middle + [high],
        middle + [high, low],
    ]


def column_groups(width):
    tiles = width // LANES
    cuts = [(tiles * g) // 3 * LANES for g in range(4)]
    return [(cuts[g], cuts[g + 1] - cuts[g]) for g in range(3)]


def gather_kernel(n, experts_axis, width, mine_ref, out_ref, *scratch):
    bits = n.bit_length() - 1
    me = flat_index(experts_axis)
    core, orders = axis_orders(n, experts_axis)
    held, send_sem, recv_sem = scratch[:3], scratch[3], scratch[4]
    for group, (first, wide) in enumerate(column_groups(width)):
        held[group][0] = mine_ref[:, first : first + wide]
    greet_bits(bits, experts_axis)
    plans = [order[::-1] + [core] for order in orders]
    for stage in range(bits):
        count = 1 << stage
        copies = []
        for group in range(3):
            bit = plans[group][stage]
            copy = pltpu.make_async_remote_copy(
                src_ref=held[group].at[pl.ds(0, count)],
                dst_ref=held[group].at[pl.ds(count, count)],
                send_sem=send_sem.at[stage, group],
                recv_sem=recv_sem.at[stage, group],
                device_id=place(flipped(me, bit), experts_axis),
                device_id_type=MESH,
            )
            copy.start()
            copies.append(copy)
        for copy in copies:
            copy.wait()
    for group, (first, wide) in enumerate(column_groups(width)):
        for slot in range(n):
            offset = sum(
                1 << plans[group][stage] for stage in range(bits) if (slot >> stage) & 1
            )
            out_ref[offset, :, first : first + wide] = held[group][slot]


def gather(mine, n, experts_axis):
    rows, width = mine.shape
    bits = n.bit_length() - 1
    return pl.pallas_call(
        functools.partial(gather_kernel, n, experts_axis, width),
        out_shape=jax.ShapeDtypeStruct((n, rows, width), mine.dtype),
        in_specs=[pl.BlockSpec(memory_space=pltpu.VMEM)],
        out_specs=pl.BlockSpec(memory_space=pltpu.VMEM),
        scratch_shapes=[
            pltpu.VMEM((n, rows, wide), mine.dtype) for _, wide in column_groups(width)
        ]
        + [pltpu.SemaphoreType.DMA((bits, 3)), pltpu.SemaphoreType.DMA((bits, 3))],
        compiler_params=pltpu.CompilerParams(
            collective_id=1, has_side_effects=True, vmem_limit_bytes=48 * 1024 * 1024
        ),
    )(mine)


def stage_types(bits):
    return [jnp.bfloat16 if stage < 3 else jnp.float32 for stage in range(bits)]


def reduce_kernel(n, experts_axis, block, width, left_ref, right_ref, out_ref, *scratch):
    bits = n.bit_length() - 1
    me = flat_index(experts_axis)
    core, orders = axis_orders(n, experts_axis)
    plans = [[core] + order for order in orders]
    groups = column_groups(width)
    types = stage_types(bits)
    kept = [[scratch[3 * (s * 3 + g)] for g in range(3)] for s in range(bits)]
    sent = [[scratch[3 * (s * 3 + g) + 1] for g in range(3)] for s in range(bits)]
    came = [[scratch[3 * (s * 3 + g) + 2] for g in range(3)] for s in range(bits)]
    send_sem, recv_sem = scratch[9 * bits], scratch[9 * bits + 1]
    greet_bits(bits, experts_axis)

    def transfer(stage, group):
        return pltpu.make_async_remote_copy(
            src_ref=sent[stage][group],
            dst_ref=came[stage][group],
            send_sem=send_sem.at[stage, group],
            recv_sem=recv_sem.at[stage, group],
            device_id=place(flipped(me, plans[group][stage]), experts_axis),
            device_id_type=MESH,
        )

    def side_of(bit):
        return (me // (1 << bit)) % 2

    chunk = experts_axis * block
    spans = n // (2 * experts_axis)

    def first_half(group, side, into, kind):
        first, wide = groups[group]
        for span in range(spans):
            at = pl.multiple_of((2 * span + side) * chunk, chunk)
            product = jnp.dot(
                left_ref[pl.ds(at, chunk), :],
                right_ref[:, first : first + wide],
                preferred_element_type=jnp.float32,
            )
            for item in range(experts_axis):
                into[span * experts_axis + item] = product[
                    item * block : (item + 1) * block
                ].astype(kind)

    for group in range(3):
        first_half(group, 1 - side_of(core), sent[0][group], types[0])
        transfer(0, group).start()
    for group in range(3):
        first_half(group, side_of(core), kept[0][group], jnp.float32)

    left = [[b for b in range(bits - 1, -1, -1) if b != core] for _ in groups]
    for stage in range(1, bits):
        half = n >> (stage + 1)
        for group in range(3):
            bit = plans[group][stage]
            low = 1 << (len(left[group]) - left[group].index(bit) - 1)
            left[group].remove(bit)
            mine = side_of(bit)

            def move(side, into, kind, low=low, stage=stage, group=group, half=half):
                def one(item, carry):
                    at = (item // low) * (2 * low) + side * low + item % low
                    into[item] = (
                        kept[stage - 1][group][at]
                        + came[stage - 1][group][at].astype(jnp.float32)
                    ).astype(kind)
                    return carry

                lax.fori_loop(0, half, one, 0)

            transfer(stage - 1, group).wait()
            move(1 - mine, sent[stage][group], types[stage])
            transfer(stage, group).start()
            move(mine, kept[stage][group], jnp.float32)
    for group, (first, wide) in enumerate(groups):
        transfer(bits - 1, group).wait()
        out_ref[:, first : first + wide] = kept[bits - 1][group][0] + came[bits - 1][group][
            0
        ].astype(jnp.float32)


def reduce_scatter(left, right, block, n, experts_axis):
    width = right.shape[1]
    bits = n.bit_length() - 1
    types = stage_types(bits)
    scratch = []
    for stage in range(bits):
        half = n >> (stage + 1)
        for _, wide in column_groups(width):
            scratch.append(pltpu.VMEM((half, block, wide), jnp.float32))
            scratch.append(pltpu.VMEM((half, block, wide), types[stage]))
            scratch.append(pltpu.VMEM((half, block, wide), types[stage]))
    return pl.pallas_call(
        functools.partial(reduce_kernel, n, experts_axis, block, width),
        out_shape=jax.ShapeDtypeStruct((block, width), jnp.float32),
        in_specs=[pl.BlockSpec(memory_space=pltpu.VMEM)] * 2,
        out_specs=pl.BlockSpec(memory_space=pltpu.VMEM),
        scratch_shapes=scratch
        + [pltpu.SemaphoreType.DMA((bits, 3)), pltpu.SemaphoreType.DMA((bits, 3))],
        compiler_params=pltpu.CompilerParams(
            collective_id=2, has_side_effects=True, vmem_limit_bytes=52 * 1024 * 1024
        ),
    )(left, right)


def lines_of(blocks, count, rows, first):
    lines = blocks.shape[0]
    wanted = jnp.arange(lines // rows * count, dtype=jnp.int32)
    wanted = wanted // count * rows + first + wanted % count
    chosen = wanted[:, None] == jnp.arange(lines, dtype=jnp.int32)[None, :]
    return jnp.dot(
        chosen.astype(jnp.bfloat16), blocks, preferred_element_type=jnp.float32
    ).astype(jnp.bfloat16)


def trunk(rows, gain, weight):
    values = rows.astype(jnp.float32)
    factor = lax.rsqrt(jnp.mean(values * values, axis=1, keepdims=True) + 1e-06)
    normed = (values * factor * gain).astype(jnp.bfloat16)
    hidden = values + jnp.dot(normed, weight, preferred_element_type=jnp.float32)
    return normed, hidden.astype(jnp.bfloat16)


def dot_t(a, b):
    return lax.dot_general(a, b, (((1,), (1,)), ((), ())), preferred_element_type=jnp.float32)


def t_dot(a, b):
    return lax.dot_general(a, b, (((0,), (0,)), ((), ())), preferred_element_type=jnp.float32)


def through_expert(hidden, cotan, gate_w, up_w, down_w):
    gate_pre = jnp.dot(hidden, gate_w, preferred_element_type=jnp.float32)
    up_pre = jnp.dot(hidden, up_w, preferred_element_type=jnp.float32)
    sigma = jax.nn.sigmoid(gate_pre)
    silu_val = gate_pre * sigma
    active = (silu_val * up_pre).astype(jnp.bfloat16)
    d_active = dot_t(cotan, down_w)
    d_gate = (d_active * up_pre * sigma * (1.0 + gate_pre * (1.0 - sigma))).astype(jnp.bfloat16)
    d_up = (d_active * silu_val).astype(jnp.bfloat16)
    d_rows = (dot_t(d_gate, gate_w) + dot_t(d_up, up_w)).astype(jnp.bfloat16)
    return active, d_gate, d_up, d_rows


def body(embeds, trunk_gain, trunk_weight, w_gate, w_up, w_down, tags, plan, helper, cotangent):
    n = lax.axis_size(("dp", "expert"))
    experts_axis = lax.axis_size("expert")
    device = flat_index(experts_axis)
    hot_expert = plan[0]
    tokens, feature = embeds.shape
    capacity = tokens // n
    hot_slots = tokens // 32
    rows = padded(2 * capacity, TILE)
    gate_w, up_w, down_w = w_gate[0], w_up[0], w_down[0]

    token = jnp.arange(tokens, dtype=jnp.int32)
    before = (helper[:, None] == helper[None, :]) & (token[:, None] > token[None, :])
    slot = jnp.sum(before.astype(jnp.int32), axis=1)
    target = helper * rows + slot
    line = jnp.arange(n * rows, dtype=jnp.int32)
    pick = jnp.concatenate(
        [line[:, None] == target[None, :], line[:, None] == target[None, :] + capacity], axis=1
    ).astype(jnp.bfloat16)
    flagged = ((tags == hot_expert) & (helper != hot_expert)).astype(jnp.bfloat16)
    flag_lanes = jnp.broadcast_to(flagged[:, None], (tokens, LANES))
    content = jnp.concatenate(
        [
            jnp.concatenate([embeds, flag_lanes], axis=1),
            jnp.concatenate([cotangent, jnp.zeros_like(flag_lanes)], axis=1),
        ],
        axis=0,
    )
    send = jnp.dot(pick, content, preferred_element_type=jnp.float32).astype(jnp.bfloat16)
    got = exchange(send.reshape(n, rows, feature + LANES), n, experts_axis)
    got = got.reshape(n * rows, feature + LANES)
    got_wide = lines_of(got, capacity, rows, 0)
    got_embeds = got_wide[:, :feature]
    got_cotan = lines_of(got[:, :feature], capacity, rows, capacity)
    flags = got_wide[:, feature] > 0

    rank = jnp.sum((flags[None, :] & (token[:, None] > token[None, :])).astype(jnp.int32), axis=1)
    picker = (rank[None, :] == jnp.arange(hot_slots, dtype=jnp.int32)[:, None]) & flags[None, :]
    picker = picker.astype(jnp.bfloat16)
    hot = jnp.concatenate(
        [
            jnp.dot(picker, got_embeds, preferred_element_type=jnp.float32),
            jnp.dot(picker, got_cotan, preferred_element_type=jnp.float32),
        ],
        axis=0,
    ).astype(jnp.bfloat16)
    pooled = gather(hot, n, experts_axis)
    pooled = pooled.reshape(n * 2 * hot_slots, feature)
    hot_embeds = lines_of(pooled, hot_slots, 2 * hot_slots, 0)
    hot_cotan = lines_of(pooled, hot_slots, 2 * hot_slots, hot_slots)
    is_owner = device == hot_expert
    hot_cotan = jnp.where(is_owner, hot_cotan, jnp.zeros_like(hot_cotan))
    own_cotan = jnp.where(flags[:, None], jnp.zeros_like(got_cotan), got_cotan)

    all_embeds = jnp.concatenate([got_embeds, hot_embeds], axis=0)
    all_cotan = jnp.concatenate([own_cotan, hot_cotan], axis=0)
    normed, hidden = trunk(all_embeds, trunk_gain, trunk_weight)
    active, d_gate, d_up, d_rows = through_expert(hidden, all_cotan, gate_w, up_w, down_w)

    share = feature // n
    block = padded(share, TILE // 2)
    column = jnp.arange(n * block, dtype=jnp.int32)
    source = jnp.where(column % block < share, column // block * share + column % block, -1)
    spread = (source[:, None] == jnp.arange(feature, dtype=jnp.int32)[None, :]).astype(
        jnp.bfloat16
    )
    normed_lines = dot_t(spread, normed).astype(jnp.bfloat16)
    grad_trunk = reduce_scatter(normed_lines, d_rows, block, n, experts_axis)[:share]

    grad_gate = t_dot(hidden, d_gate).astype(jnp.bfloat16)[None]
    grad_up = t_dot(hidden, d_up).astype(jnp.bfloat16)[None]
    grad_down = t_dot(active, all_cotan).astype(jnp.bfloat16)[None]
    return (grad_gate, grad_up, grad_down, grad_trunk)


def solution(mesh):
    spread_rows = P(("dp", "expert"), None)
    spread_first = P(("dp", "expert"), None, None)
    return jax.shard_map(
        body,
        mesh=mesh,
        in_specs=(
            spread_rows,
            P(),
            P(),
            spread_first,
            spread_first,
            spread_first,
            P(("dp", "expert")),
            P(),
            P(("dp", "expert")),
            spread_rows,
        ),
        out_specs=(spread_first, spread_first, spread_first, spread_rows),
        check_vma=False,
    )
```

```python
import functools

import jax
import jax.numpy as jnp
from jax import lax
from jax.experimental import pallas as pl
from jax.experimental.pallas import tpu as pltpu
from jax.sharding import PartitionSpec as P

LANES = 128
TILE = 16
MESH = pl.DeviceIdType.MESH


def padded(value, multiple):
    return -(-value // multiple) * multiple


def flat_index(experts_axis):
    return lax.axis_index("dp") * experts_axis + lax.axis_index("expert")


def place(flat, experts_axis):
    return (flat // experts_axis, flat % experts_axis)


def flipped(me, bit):
    weight = 1 << bit
    return me + (1 - 2 * ((me // weight) % 2)) * weight


def greet_all(n, experts_axis):
    me = flat_index(experts_axis)
    barrier = pltpu.get_barrier_semaphore()

    def greet(step, carry):
        pl.semaphore_signal(
            barrier,
            inc=1,
            device_id=place(lax.rem(me + step, n), experts_axis),
            device_id_type=MESH,
        )
        return carry

    lax.fori_loop(1, n, greet, 0)
    pl.semaphore_wait(barrier, n - 1)


def greet_bits(bits, experts_axis):
    me = flat_index(experts_axis)
    barrier = pltpu.get_barrier_semaphore()
    for bit in range(bits):
        pl.semaphore_signal(
            barrier, inc=1, device_id=place(flipped(me, bit), experts_axis), device_id_type=MESH
        )
    pl.semaphore_wait(barrier, bits)


def exchange_kernel(n, experts_axis, send_ref, out_ref, send_sem, recv_sem, own_sem):
    me = flat_index(experts_axis)
    greet_all(n, experts_axis)
    own = pltpu.make_async_copy(send_ref.at[me], out_ref.at[me], own_sem)
    own.start()

    def copy_to(step):
        to = lax.rem(me + step, n)
        return pltpu.make_async_remote_copy(
            src_ref=send_ref.at[to],
            dst_ref=out_ref.at[me],
            send_sem=send_sem.at[to],
            recv_sem=recv_sem.at[me],
            device_id=place(to, experts_axis),
            device_id_type=MESH,
        )

    def copy_from(step):
        source = lax.rem(me + step, n)
        return pltpu.make_async_remote_copy(
            src_ref=send_ref.at[source],
            dst_ref=out_ref.at[source],
            send_sem=send_sem.at[source],
            recv_sem=recv_sem.at[source],
            device_id=place(source, experts_axis),
            device_id_type=MESH,
        )

    def start(step, carry):
        copy_to(step).start()
        return carry

    def finish(step, carry):
        copy = copy_from(step)
        copy.wait_send()
        copy.wait_recv()
        return carry

    lax.fori_loop(1, n, start, 0)
    own.wait()
    lax.fori_loop(1, n, finish, 0)


def exchange(send, n, experts_axis):
    return pl.pallas_call(
        functools.partial(exchange_kernel, n, experts_axis),
        out_shape=jax.ShapeDtypeStruct(send.shape, send.dtype),
        in_specs=[pl.BlockSpec(memory_space=pltpu.VMEM)],
        out_specs=pl.BlockSpec(memory_space=pltpu.VMEM),
        scratch_shapes=[
            pltpu.SemaphoreType.DMA((n,)),
            pltpu.SemaphoreType.DMA((n,)),
            pltpu.SemaphoreType.DMA,
        ],
        compiler_params=pltpu.CompilerParams(
            collective_id=0, has_side_effects=True, vmem_limit_bytes=40 * 1024 * 1024
        ),
    )(send)


def axis_orders(n, experts_axis):
    bits = n.bit_length() - 1
    core = experts_axis.bit_length() - 1
    others = [b for b in range(bits) if b != core]
    low = others[0]
    high = others[-1]
    middle = others[1:-1]
    return core, [
        [high, low] + middle,
        [low] + middle + [high],
        middle + [high, low],
    ]


def column_groups(width):
    tiles = width // LANES
    cuts = [(tiles * g) // 3 * LANES for g in range(4)]
    return [(cuts[g], cuts[g + 1] - cuts[g]) for g in range(3)]


def tile_of(width):
    tile = 3 * LANES
    while width % tile:
        tile -= LANES
    return tile


def contract_last(a, b):
    return lax.dot_general(a, b, (((1,), (1,)), ((), ())), preferred_element_type=jnp.float32)


def own_steps(ins, outs):
    rows_ref, cotan_ref, gain_ref, trunk_ref, gate_ref, up_ref, down_ref = ins
    normed_ref, hidden_ref, act_ref, dgate_ref, dup_ref, drows_ref = outs
    feature = rows_ref.shape[1]
    units = gate_ref.shape[1]
    wide = tile_of(feature)
    deep = tile_of(units)

    def trunk_step():
        values = rows_ref[...].astype(jnp.float32)
        factor = lax.rsqrt(jnp.mean(values * values, axis=1, keepdims=True) + 1e-06)
        normed_ref[...] = (values * factor * gain_ref[...]).astype(jnp.bfloat16)

        def one(tile, carry):
            at = pl.ds(pl.multiple_of(tile * wide, wide), wide)
            hidden_ref[:, at] = (
                rows_ref[:, at].astype(jnp.float32)
                + jnp.dot(normed_ref[...], trunk_ref[:, at], preferred_element_type=jnp.float32)
            ).astype(jnp.bfloat16)
            return carry

        lax.fori_loop(0, feature // wide, one, 0)

    def expert_step(first, last):
        def one(tile, carry):
            at = pl.ds(pl.multiple_of(tile * deep, deep), deep)
            gate_pre = jnp.dot(
                hidden_ref[...], gate_ref[:, at], preferred_element_type=jnp.float32
            )
            up_pre = jnp.dot(hidden_ref[...], up_ref[:, at], preferred_element_type=jnp.float32)
            sigma = jax.nn.sigmoid(gate_pre)
            silu_val = gate_pre * sigma
            d_active = contract_last(cotan_ref[...], down_ref[at, :])
            act_ref[:, at] = (silu_val * up_pre).astype(jnp.bfloat16)
            dgate_ref[:, at] = (
                d_active * up_pre * sigma * (1.0 + gate_pre * (1.0 - sigma))
            ).astype(jnp.bfloat16)
            dup_ref[:, at] = (d_active * silu_val).astype(jnp.bfloat16)
            return carry

        lax.fori_loop(first, last, one, 0)

    def rows_step():
        def one(tile, carry):
            at = pl.ds(pl.multiple_of(tile * wide, wide), wide)
            drows_ref[:, at] = (
                contract_last(dgate_ref[...], gate_ref[at, :])
                + contract_last(dup_ref[...], up_ref[at, :])
            ).astype(jnp.bfloat16)
            return carry

        lax.fori_loop(0, feature // wide, one, 0)

    tiles = units // deep
    return [
        trunk_step,
        lambda: expert_step(0, tiles // 2),
        lambda: expert_step(tiles // 2, tiles),
        rows_step,
    ]


def gather_kernel(n, experts_axis, width, mine_ref, *refs):
    bits = n.bit_length() - 1
    ins, out_ref, outs, scratch = refs[:7], refs[7], refs[8:14], refs[14:]
    me = flat_index(experts_axis)
    core, orders = axis_orders(n, experts_axis)
    held, send_sem, recv_sem = scratch[:3], scratch[3], scratch[4]
    for group, (first, wide) in enumerate(column_groups(width)):
        held[group][0] = mine_ref[:, first : first + wide]
    greet_bits(bits, experts_axis)
    plans = [order[::-1] + [core] for order in orders]
    steps = own_steps(ins, outs)
    for stage in range(bits):
        count = 1 << stage
        copies = []
        for group in range(3):
            bit = plans[group][stage]
            copy = pltpu.make_async_remote_copy(
                src_ref=held[group].at[pl.ds(0, count)],
                dst_ref=held[group].at[pl.ds(count, count)],
                send_sem=send_sem.at[stage, group],
                recv_sem=recv_sem.at[stage, group],
                device_id=place(flipped(me, bit), experts_axis),
                device_id_type=MESH,
            )
            copy.start()
            copies.append(copy)
        if stage < len(steps):
            steps[stage]()
        for copy in copies:
            copy.wait()
    for group, (first, wide) in enumerate(column_groups(width)):
        for slot in range(n):
            offset = sum(
                1 << plans[group][stage] for stage in range(bits) if (slot >> stage) & 1
            )
            out_ref[offset, :, first : first + wide] = held[group][slot]


def gather(mine, own, n, experts_axis):
    rows, width = mine.shape
    bits = n.bit_length() - 1
    tokens, units = own[0].shape[0], own[4].shape[1]
    shapes = [(n, rows, width), (tokens, width), (tokens, width)]
    shapes += [(tokens, units)] * 3 + [(tokens, width)]
    return pl.pallas_call(
        functools.partial(gather_kernel, n, experts_axis, width),
        out_shape=[jax.ShapeDtypeStruct(shape, mine.dtype) for shape in shapes],
        in_specs=[pl.BlockSpec(memory_space=pltpu.VMEM)] * 8,
        out_specs=[pl.BlockSpec(memory_space=pltpu.VMEM)] * 7,
        scratch_shapes=[
            pltpu.VMEM((n, rows, wide), mine.dtype) for _, wide in column_groups(width)
        ]
        + [pltpu.SemaphoreType.DMA((bits, 3)), pltpu.SemaphoreType.DMA((bits, 3))],
        compiler_params=pltpu.CompilerParams(
            collective_id=1, has_side_effects=True, vmem_limit_bytes=48 * 1024 * 1024
        ),
    )(mine, *own)


def stage_types(bits):
    return [jnp.bfloat16 if stage < 3 else jnp.float32 for stage in range(bits)]


def reduce_kernel(n, experts_axis, block, width, left_ref, right_ref, out_ref, *scratch):
    bits = n.bit_length() - 1
    me = flat_index(experts_axis)
    core, orders = axis_orders(n, experts_axis)
    plans = [[core] + order for order in orders]
    groups = column_groups(width)
    types = stage_types(bits)
    kept = [[scratch[3 * (s * 3 + g)] for g in range(3)] for s in range(bits)]
    sent = [[scratch[3 * (s * 3 + g) + 1] for g in range(3)] for s in range(bits)]
    came = [[scratch[3 * (s * 3 + g) + 2] for g in range(3)] for s in range(bits)]
    send_sem, recv_sem = scratch[9 * bits], scratch[9 * bits + 1]
    greet_bits(bits, experts_axis)

    def transfer(stage, group):
        return pltpu.make_async_remote_copy(
            src_ref=sent[stage][group],
            dst_ref=came[stage][group],
            send_sem=send_sem.at[stage, group],
            recv_sem=recv_sem.at[stage, group],
            device_id=place(flipped(me, plans[group][stage]), experts_axis),
            device_id_type=MESH,
        )

    def side_of(bit):
        return (me // (1 << bit)) % 2

    chunk = experts_axis * block
    spans = n // (2 * experts_axis)

    def first_half(group, side, into, kind):
        first, wide = groups[group]
        for span in range(spans):
            at = pl.multiple_of((2 * span + side) * chunk, chunk)
            product = jnp.dot(
                left_ref[pl.ds(at, chunk), :],
                right_ref[:, first : first + wide],
                preferred_element_type=jnp.float32,
            )
            for item in range(experts_axis):
                into[span * experts_axis + item] = product[
                    item * block : (item + 1) * block
                ].astype(kind)

    for group in range(3):
        first_half(group, 1 - side_of(core), sent[0][group], types[0])
        transfer(0, group).start()
    for group in range(3):
        first_half(group, side_of(core), kept[0][group], jnp.float32)

    left = [[b for b in range(bits - 1, -1, -1) if b != core] for _ in groups]
    for stage in range(1, bits):
        half = n >> (stage + 1)
        for group in range(3):
            bit = plans[group][stage]
            low = 1 << (len(left[group]) - left[group].index(bit) - 1)
            left[group].remove(bit)
            mine = side_of(bit)

            def move(side, into, kind, low=low, stage=stage, group=group, half=half):
                def one(item, carry):
                    at = (item // low) * (2 * low) + side * low + item % low
                    into[item] = (
                        kept[stage - 1][group][at]
                        + came[stage - 1][group][at].astype(jnp.float32)
                    ).astype(kind)
                    return carry

                lax.fori_loop(0, half, one, 0)

            transfer(stage - 1, group).wait()
            move(1 - mine, sent[stage][group], types[stage])
            transfer(stage, group).start()
            move(mine, kept[stage][group], jnp.float32)
    for group, (first, wide) in enumerate(groups):
        transfer(bits - 1, group).wait()
        out_ref[:, first : first + wide] = kept[bits - 1][group][0] + came[bits - 1][group][
            0
        ].astype(jnp.float32)


def reduce_scatter(left, right, block, n, experts_axis):
    width = right.shape[1]
    bits = n.bit_length() - 1
    types = stage_types(bits)
    scratch = []
    for stage in range(bits):
        half = n >> (stage + 1)
        for _, wide in column_groups(width):
            scratch.append(pltpu.VMEM((half, block, wide), jnp.float32))
            scratch.append(pltpu.VMEM((half, block, wide), types[stage]))
            scratch.append(pltpu.VMEM((half, block, wide), types[stage]))
    return pl.pallas_call(
        functools.partial(reduce_kernel, n, experts_axis, block, width),
        out_shape=jax.ShapeDtypeStruct((block, width), jnp.float32),
        in_specs=[pl.BlockSpec(memory_space=pltpu.VMEM)] * 2,
        out_specs=pl.BlockSpec(memory_space=pltpu.VMEM),
        scratch_shapes=scratch
        + [pltpu.SemaphoreType.DMA((bits, 3)), pltpu.SemaphoreType.DMA((bits, 3))],
        compiler_params=pltpu.CompilerParams(
            collective_id=2, has_side_effects=True, vmem_limit_bytes=52 * 1024 * 1024
        ),
    )(left, right)


def lines_of(blocks, count, rows, first):
    lines = blocks.shape[0]
    wanted = jnp.arange(lines // rows * count, dtype=jnp.int32)
    wanted = wanted // count * rows + first + wanted % count
    chosen = wanted[:, None] == jnp.arange(lines, dtype=jnp.int32)[None, :]
    return jnp.dot(
        chosen.astype(jnp.bfloat16), blocks, preferred_element_type=jnp.float32
    ).astype(jnp.bfloat16)


def trunk(rows, gain, weight):
    values = rows.astype(jnp.float32)
    factor = lax.rsqrt(jnp.mean(values * values, axis=1, keepdims=True) + 1e-06)
    normed = (values * factor * gain).astype(jnp.bfloat16)
    hidden = values + jnp.dot(normed, weight, preferred_element_type=jnp.float32)
    return normed, hidden.astype(jnp.bfloat16)


def dot_t(a, b):
    return lax.dot_general(a, b, (((1,), (1,)), ((), ())), preferred_element_type=jnp.float32)


def t_dot(a, b):
    return lax.dot_general(a, b, (((0,), (0,)), ((), ())), preferred_element_type=jnp.float32)


def through_expert(hidden, cotan, gate_w, up_w, down_w):
    gate_pre = jnp.dot(hidden, gate_w, preferred_element_type=jnp.float32)
    up_pre = jnp.dot(hidden, up_w, preferred_element_type=jnp.float32)
    sigma = jax.nn.sigmoid(gate_pre)
    silu_val = gate_pre * sigma
    active = (silu_val * up_pre).astype(jnp.bfloat16)
    d_active = dot_t(cotan, down_w)
    d_gate = (d_active * up_pre * sigma * (1.0 + gate_pre * (1.0 - sigma))).astype(jnp.bfloat16)
    d_up = (d_active * silu_val).astype(jnp.bfloat16)
    d_rows = (dot_t(d_gate, gate_w) + dot_t(d_up, up_w)).astype(jnp.bfloat16)
    return active, d_gate, d_up, d_rows


def body(embeds, trunk_gain, trunk_weight, w_gate, w_up, w_down, tags, plan, helper, cotangent):
    n = lax.axis_size(("dp", "expert"))
    experts_axis = lax.axis_size("expert")
    device = flat_index(experts_axis)
    hot_expert = plan[0]
    tokens, feature = embeds.shape
    capacity = tokens // n
    hot_slots = tokens // 32
    rows = padded(2 * capacity, TILE)
    gate_w, up_w, down_w = w_gate[0], w_up[0], w_down[0]

    token = jnp.arange(tokens, dtype=jnp.int32)
    before = (helper[:, None] == helper[None, :]) & (token[:, None] > token[None, :])
    slot = jnp.sum(before.astype(jnp.int32), axis=1)
    target = helper * rows + slot
    line = jnp.arange(n * rows, dtype=jnp.int32)
    pick = jnp.concatenate(
        [line[:, None] == target[None, :], line[:, None] == target[None, :] + capacity], axis=1
    ).astype(jnp.bfloat16)
    flagged = ((tags == hot_expert) & (helper != hot_expert)).astype(jnp.bfloat16)
    flag_lanes = jnp.broadcast_to(flagged[:, None], (tokens, LANES))
    content = jnp.concatenate(
        [
            jnp.concatenate([embeds, flag_lanes], axis=1),
            jnp.concatenate([cotangent, jnp.zeros_like(flag_lanes)], axis=1),
        ],
        axis=0,
    )
    send = jnp.dot(pick, content, preferred_element_type=jnp.float32).astype(jnp.bfloat16)
    got = exchange(send.reshape(n, rows, feature + LANES), n, experts_axis)
    got = got.reshape(n * rows, feature + LANES)
    got_wide = lines_of(got, capacity, rows, 0)
    got_embeds = got_wide[:, :feature]
    got_cotan = lines_of(got[:, :feature], capacity, rows, capacity)
    flags = got_wide[:, feature] > 0

    rank = jnp.sum((flags[None, :] & (token[:, None] > token[None, :])).astype(jnp.int32), axis=1)
    picker = (rank[None, :] == jnp.arange(hot_slots, dtype=jnp.int32)[:, None]) & flags[None, :]
    picker = picker.astype(jnp.bfloat16)
    hot = jnp.concatenate(
        [
            jnp.dot(picker, got_embeds, preferred_element_type=jnp.float32),
            jnp.dot(picker, got_cotan, preferred_element_type=jnp.float32),
        ],
        axis=0,
    ).astype(jnp.bfloat16)
    own_cotan = jnp.where(flags[:, None], jnp.zeros_like(got_cotan), got_cotan)
    own = (got_embeds, own_cotan, trunk_gain[None], trunk_weight, gate_w, up_w, down_w)
    pooled, *own_parts = gather(hot, own, n, experts_axis)
    pooled = pooled.reshape(n * 2 * hot_slots, feature)
    hot_embeds = lines_of(pooled, hot_slots, 2 * hot_slots, 0)
    hot_cotan = lines_of(pooled, hot_slots, 2 * hot_slots, hot_slots)
    is_owner = device == hot_expert
    hot_cotan = jnp.where(is_owner, hot_cotan, jnp.zeros_like(hot_cotan))
    hot_parts = trunk(hot_embeds, trunk_gain, trunk_weight)
    hot_parts = hot_parts + through_expert(hot_parts[1], hot_cotan, gate_w, up_w, down_w)
    normed, hidden, active, d_gate, d_up, d_rows = [
        jnp.concatenate([a, b], axis=0) for a, b in zip(own_parts, hot_parts)
    ]
    all_cotan = jnp.concatenate([own_cotan, hot_cotan], axis=0)

    share = feature // n
    block = padded(share, TILE // 2)
    column = jnp.arange(n * block, dtype=jnp.int32)
    source = jnp.where(column % block < share, column // block * share + column % block, -1)
    spread = (source[:, None] == jnp.arange(feature, dtype=jnp.int32)[None, :]).astype(
        jnp.bfloat16
    )
    normed_lines = dot_t(spread, normed).astype(jnp.bfloat16)
    grad_trunk = reduce_scatter(normed_lines, d_rows, block, n, experts_axis)[:share]

    grad_gate = t_dot(hidden, d_gate).astype(jnp.bfloat16)[None]
    grad_up = t_dot(hidden, d_up).astype(jnp.bfloat16)[None]
    grad_down = t_dot(active, all_cotan).astype(jnp.bfloat16)[None]
    return (grad_gate, grad_up, grad_down, grad_trunk)


def solution(mesh):
    spread_rows = P(("dp", "expert"), None)
    spread_first = P(("dp", "expert"), None, None)
    return jax.shard_map(
        body,
        mesh=mesh,
        in_specs=(
            spread_rows,
            P(),
            P(),
            spread_first,
            spread_first,
            spread_first,
            P(("dp", "expert")),
            P(),
            P(("dp", "expert")),
            spread_rows,
        ),
        out_specs=(spread_first, spread_first, spread_first, spread_rows),
        check_vma=False,
    )
```

```python
import functools

import jax
import jax.numpy as jnp
from jax import lax
from jax.experimental import pallas as pl
from jax.experimental.pallas import tpu as pltpu
from jax.sharding import PartitionSpec as P

LANES = 128
TILE = 16
MESH = pl.DeviceIdType.MESH


def padded(value, multiple):
    return -(-value // multiple) * multiple


def flat_index(experts_axis):
    return lax.axis_index("dp") * experts_axis + lax.axis_index("expert")


def place(flat, experts_axis):
    return (flat // experts_axis, flat % experts_axis)


def flipped(me, bit):
    weight = 1 << bit
    return me + (1 - 2 * ((me // weight) % 2)) * weight


def greet_all(n, experts_axis):
    me = flat_index(experts_axis)
    barrier = pltpu.get_barrier_semaphore()

    def greet(step, carry):
        pl.semaphore_signal(
            barrier,
            inc=1,
            device_id=place(lax.rem(me + step, n), experts_axis),
            device_id_type=MESH,
        )
        return carry

    lax.fori_loop(1, n, greet, 0)
    pl.semaphore_wait(barrier, n - 1)


def greet_bits(bits, experts_axis):
    me = flat_index(experts_axis)
    barrier = pltpu.get_barrier_semaphore()
    for bit in range(bits):
        pl.semaphore_signal(
            barrier, inc=1, device_id=place(flipped(me, bit), experts_axis), device_id_type=MESH
        )
    pl.semaphore_wait(barrier, bits)


def exchange_kernel(
    n, experts_axis, send_ref, mark_ref, out_ref, seen_ref, send_sem, recv_sem, small_send, small_recv, own_sem
):
    me = flat_index(experts_axis)
    greet_all(n, experts_axis)
    own = pltpu.make_async_copy(send_ref.at[me], out_ref.at[me], own_sem)
    own.start()
    seen_ref[me] = mark_ref[me]

    def mark_to(step):
        to = lax.rem(me + step, n)
        return pltpu.make_async_remote_copy(
            src_ref=mark_ref.at[to],
            dst_ref=seen_ref.at[me],
            send_sem=small_send.at[to],
            recv_sem=small_recv.at[me],
            device_id=place(to, experts_axis),
            device_id_type=MESH,
        )

    def mark_from(step):
        source = lax.rem(me + step, n)
        return pltpu.make_async_remote_copy(
            src_ref=mark_ref.at[source],
            dst_ref=seen_ref.at[source],
            send_sem=small_send.at[source],
            recv_sem=small_recv.at[source],
            device_id=place(source, experts_axis),
            device_id_type=MESH,
        )

    def copy_to(step):
        to = lax.rem(me + step, n)
        return pltpu.make_async_remote_copy(
            src_ref=send_ref.at[to],
            dst_ref=out_ref.at[me],
            send_sem=send_sem.at[to],
            recv_sem=recv_sem.at[me],
            device_id=place(to, experts_axis),
            device_id_type=MESH,
        )

    def copy_from(step):
        source = lax.rem(me + step, n)
        return pltpu.make_async_remote_copy(
            src_ref=send_ref.at[source],
            dst_ref=out_ref.at[source],
            send_sem=send_sem.at[source],
            recv_sem=recv_sem.at[source],
            device_id=place(source, experts_axis),
            device_id_type=MESH,
        )

    def start(step, carry):
        copy_to(step).start()
        mark_to(step).start()
        return carry

    def finish(step, carry):
        copy = copy_from(step)
        copy.wait_send()
        copy.wait_recv()
        mark = mark_from(step)
        mark.wait_send()
        mark.wait_recv()
        return carry

    lax.fori_loop(1, n, start, 0)
    own.wait()
    lax.fori_loop(1, n, finish, 0)


def exchange(send, marks, n, experts_axis):
    return pl.pallas_call(
        functools.partial(exchange_kernel, n, experts_axis),
        out_shape=[
            jax.ShapeDtypeStruct(send.shape, send.dtype),
            jax.ShapeDtypeStruct(marks.shape, marks.dtype),
        ],
        in_specs=[pl.BlockSpec(memory_space=pltpu.VMEM)] * 2,
        out_specs=[pl.BlockSpec(memory_space=pltpu.VMEM)] * 2,
        scratch_shapes=[
            pltpu.SemaphoreType.DMA((n,)),
            pltpu.SemaphoreType.DMA((n,)),
            pltpu.SemaphoreType.DMA((n,)),
            pltpu.SemaphoreType.DMA((n,)),
            pltpu.SemaphoreType.DMA,
        ],
        compiler_params=pltpu.CompilerParams(
            collective_id=0, has_side_effects=True, vmem_limit_bytes=40 * 1024 * 1024
        ),
    )(send, marks)


def axis_orders(n, experts_axis):
    bits = n.bit_length() - 1
    core = experts_axis.bit_length() - 1
    others = [b for b in range(bits) if b != core]
    low = others[0]
    high = others[-1]
    middle = others[1:-1]
    return core, [
        [high, low] + middle,
        [low] + middle + [high],
        middle + [high, low],
    ]


def column_groups(width):
    tiles = width // LANES
    cuts = [(tiles * g) // 3 * LANES for g in range(4)]
    return [(cuts[g], cuts[g + 1] - cuts[g]) for g in range(3)]


def gather_kernel(n, experts_axis, width, mine_ref, out_ref, *scratch):
    bits = n.bit_length() - 1
    me = flat_index(experts_axis)
    core, orders = axis_orders(n, experts_axis)
    held, send_sem, recv_sem = scratch[:3], scratch[3], scratch[4]
    for group, (first, wide) in enumerate(column_groups(width)):
        held[group][0] = mine_ref[:, first : first + wide]
    greet_bits(bits, experts_axis)
    plans = [order[::-1] + [core] for order in orders]
    for stage in range(bits):
        count = 1 << stage
        copies = []
        for group in range(3):
            bit = plans[group][stage]
            copy = pltpu.make_async_remote_copy(
                src_ref=held[group].at[pl.ds(0, count)],
                dst_ref=held[group].at[pl.ds(count, count)],
                send_sem=send_sem.at[stage, group],
                recv_sem=recv_sem.at[stage, group],
                device_id=place(flipped(me, bit), experts_axis),
                device_id_type=MESH,
            )
            copy.start()
            copies.append(copy)
        for copy in copies:
            copy.wait()
    for group, (first, wide) in enumerate(column_groups(width)):
        for slot in range(n):
            offset = sum(
                1 << plans[group][stage] for stage in range(bits) if (slot >> stage) & 1
            )
            out_ref[offset, :, first : first + wide] = held[group][slot]


def gather(mine, n, experts_axis):
    rows, width = mine.shape
    bits = n.bit_length() - 1
    return pl.pallas_call(
        functools.partial(gather_kernel, n, experts_axis, width),
        out_shape=jax.ShapeDtypeStruct((n, rows, width), mine.dtype),
        in_specs=[pl.BlockSpec(memory_space=pltpu.VMEM)],
        out_specs=pl.BlockSpec(memory_space=pltpu.VMEM),
        scratch_shapes=[
            pltpu.VMEM((n, rows, wide), mine.dtype) for _, wide in column_groups(width)
        ]
        + [pltpu.SemaphoreType.DMA((bits, 3)), pltpu.SemaphoreType.DMA((bits, 3))],
        compiler_params=pltpu.CompilerParams(
            collective_id=1, has_side_effects=True, vmem_limit_bytes=48 * 1024 * 1024
        ),
    )(mine)


def stage_types(bits):
    return [jnp.bfloat16 if stage < 3 else jnp.float32 for stage in range(bits)]


def reduce_kernel(n, experts_axis, block, width, left_ref, right_ref, out_ref, *scratch):
    bits = n.bit_length() - 1
    me = flat_index(experts_axis)
    core, orders = axis_orders(n, experts_axis)
    plans = [[core] + order for order in orders]
    groups = column_groups(width)
    types = stage_types(bits)
    kept = [[scratch[3 * (s * 3 + g)] for g in range(3)] for s in range(bits)]
    sent = [[scratch[3 * (s * 3 + g) + 1] for g in range(3)] for s in range(bits)]
    came = [[scratch[3 * (s * 3 + g) + 2] for g in range(3)] for s in range(bits)]
    send_sem, recv_sem = scratch[9 * bits], scratch[9 * bits + 1]
    greet_bits(bits, experts_axis)

    def transfer(stage, group):
        return pltpu.make_async_remote_copy(
            src_ref=sent[stage][group],
            dst_ref=came[stage][group],
            send_sem=send_sem.at[stage, group],
            recv_sem=recv_sem.at[stage, group],
            device_id=place(flipped(me, plans[group][stage]), experts_axis),
            device_id_type=MESH,
        )

    def side_of(bit):
        return (me // (1 << bit)) % 2

    chunk = experts_axis * block
    spans = n // (2 * experts_axis)

    def first_half(group, side, into, kind):
        first, wide = groups[group]
        for span in range(spans):
            at = pl.multiple_of((2 * span + side) * chunk, chunk)
            product = jnp.dot(
                left_ref[pl.ds(at, chunk), :],
                right_ref[:, first : first + wide],
                preferred_element_type=jnp.float32,
            )
            for item in range(experts_axis):
                into[span * experts_axis + item] = product[
                    item * block : (item + 1) * block
                ].astype(kind)

    for group in range(3):
        first_half(group, 1 - side_of(core), sent[0][group], types[0])
        transfer(0, group).start()
    for group in range(3):
        first_half(group, side_of(core), kept[0][group], jnp.float32)

    left = [[b for b in range(bits - 1, -1, -1) if b != core] for _ in groups]
    for stage in range(1, bits):
        half = n >> (stage + 1)
        for group in range(3):
            bit = plans[group][stage]
            low = 1 << (len(left[group]) - left[group].index(bit) - 1)
            left[group].remove(bit)
            mine = side_of(bit)

            def move(side, into, kind, low=low, stage=stage, group=group, half=half):
                def one(item, carry):
                    at = (item // low) * (2 * low) + side * low + item % low
                    into[item] = (
                        kept[stage - 1][group][at]
                        + came[stage - 1][group][at].astype(jnp.float32)
                    ).astype(kind)
                    return carry

                lax.fori_loop(0, half, one, 0)

            transfer(stage - 1, group).wait()
            move(1 - mine, sent[stage][group], types[stage])
            transfer(stage, group).start()
            move(mine, kept[stage][group], jnp.float32)
    for group, (first, wide) in enumerate(groups):
        transfer(bits - 1, group).wait()
        out_ref[:, first : first + wide] = kept[bits - 1][group][0] + came[bits - 1][group][
            0
        ].astype(jnp.float32)


def reduce_scatter(left, right, block, n, experts_axis):
    width = right.shape[1]
    bits = n.bit_length() - 1
    types = stage_types(bits)
    scratch = []
    for stage in range(bits):
        half = n >> (stage + 1)
        for _, wide in column_groups(width):
            scratch.append(pltpu.VMEM((half, block, wide), jnp.float32))
            scratch.append(pltpu.VMEM((half, block, wide), types[stage]))
            scratch.append(pltpu.VMEM((half, block, wide), types[stage]))
    return pl.pallas_call(
        functools.partial(reduce_kernel, n, experts_axis, block, width),
        out_shape=jax.ShapeDtypeStruct((block, width), jnp.float32),
        in_specs=[pl.BlockSpec(memory_space=pltpu.VMEM)] * 2,
        out_specs=pl.BlockSpec(memory_space=pltpu.VMEM),
        scratch_shapes=scratch
        + [pltpu.SemaphoreType.DMA((bits, 3)), pltpu.SemaphoreType.DMA((bits, 3))],
        compiler_params=pltpu.CompilerParams(
            collective_id=2, has_side_effects=True, vmem_limit_bytes=52 * 1024 * 1024
        ),
    )(left, right)


def lines_of(blocks, count, rows, first):
    lines = blocks.shape[0]
    wanted = jnp.arange(lines // rows * count, dtype=jnp.int32)
    wanted = wanted // count * rows + first + wanted % count
    chosen = wanted[:, None] == jnp.arange(lines, dtype=jnp.int32)[None, :]
    return jnp.dot(
        chosen.astype(jnp.bfloat16), blocks, preferred_element_type=jnp.float32
    ).astype(jnp.bfloat16)


def trunk(rows, gain, weight):
    values = rows.astype(jnp.float32)
    factor = lax.rsqrt(jnp.mean(values * values, axis=1, keepdims=True) + 1e-06)
    normed = (values * factor * gain).astype(jnp.bfloat16)
    hidden = values + jnp.dot(normed, weight, preferred_element_type=jnp.float32)
    return normed, hidden.astype(jnp.bfloat16)


def dot_t(a, b):
    return lax.dot_general(a, b, (((1,), (1,)), ((), ())), preferred_element_type=jnp.float32)


def t_dot(a, b):
    return lax.dot_general(a, b, (((0,), (0,)), ((), ())), preferred_element_type=jnp.float32)


def through_expert(hidden, cotan, gate_w, up_w, down_w):
    gate_pre = jnp.dot(hidden, gate_w, preferred_element_type=jnp.float32)
    up_pre = jnp.dot(hidden, up_w, preferred_element_type=jnp.float32)
    sigma = jax.nn.sigmoid(gate_pre)
    silu_val = gate_pre * sigma
    active = (silu_val * up_pre).astype(jnp.bfloat16)
    d_active = dot_t(cotan, down_w)
    d_gate = (d_active * up_pre * sigma * (1.0 + gate_pre * (1.0 - sigma))).astype(jnp.bfloat16)
    d_up = (d_active * silu_val).astype(jnp.bfloat16)
    d_rows = (dot_t(d_gate, gate_w) + dot_t(d_up, up_w)).astype(jnp.bfloat16)
    return active, d_gate, d_up, d_rows


def body(embeds, trunk_gain, trunk_weight, w_gate, w_up, w_down, tags, plan, helper, cotangent):
    n = lax.axis_size(("dp", "expert"))
    experts_axis = lax.axis_size("expert")
    device = flat_index(experts_axis)
    hot_expert = plan[0]
    tokens, feature = embeds.shape
    capacity = tokens // n
    hot_slots = tokens // 32
    rows = padded(2 * capacity, TILE)
    gate_w, up_w, down_w = w_gate[0], w_up[0], w_down[0]

    token = jnp.arange(tokens, dtype=jnp.int32)
    before = (helper[:, None] == helper[None, :]) & (token[:, None] > token[None, :])
    slot = jnp.sum(before.astype(jnp.int32), axis=1)
    target = helper * rows + slot
    line = jnp.arange(n * rows, dtype=jnp.int32)
    pick = jnp.concatenate(
        [line[:, None] == target[None, :], line[:, None] == target[None, :] + capacity], axis=1
    ).astype(jnp.bfloat16)
    flagged = ((tags == hot_expert) & (helper != hot_expert)).astype(jnp.bfloat16)
    lane = jnp.arange(LANES, dtype=jnp.int32)
    to_device = (helper[None, :] == jnp.arange(n, dtype=jnp.int32)[:, None]).astype(jnp.bfloat16)
    at_lane = (slot[:, None] == lane[None, :]).astype(jnp.bfloat16) * flagged[:, None]
    marks = jnp.dot(to_device, at_lane, preferred_element_type=jnp.float32)
    content = jnp.concatenate([embeds, cotangent], axis=0)
    send = jnp.dot(pick, content, preferred_element_type=jnp.float32).astype(jnp.bfloat16)
    got, seen = exchange(
        send.reshape(n, rows, feature), marks.reshape(n, 1, LANES), n, experts_axis
    )
    got = got.reshape(n * rows, feature)
    got_embeds = lines_of(got, capacity, rows, 0)
    got_cotan = lines_of(got, capacity, rows, capacity)
    flags = seen[:, 0, :capacity].reshape(tokens) > 0

    rank = jnp.sum((flags[None, :] & (token[:, None] > token[None, :])).astype(jnp.int32), axis=1)
    picker = (rank[None, :] == jnp.arange(hot_slots, dtype=jnp.int32)[:, None]) & flags[None, :]
    picker = picker.astype(jnp.bfloat16)
    hot = jnp.concatenate(
        [
            jnp.dot(picker, got_embeds, preferred_element_type=jnp.float32),
            jnp.dot(picker, got_cotan, preferred_element_type=jnp.float32),
        ],
        axis=0,
    ).astype(jnp.bfloat16)
    pooled = gather(hot, n, experts_axis)
    pooled = pooled.reshape(n * 2 * hot_slots, feature)
    hot_embeds = lines_of(pooled, hot_slots, 2 * hot_slots, 0)
    hot_cotan = lines_of(pooled, hot_slots, 2 * hot_slots, hot_slots)
    is_owner = device == hot_expert
    hot_cotan = jnp.where(is_owner, hot_cotan, jnp.zeros_like(hot_cotan))
    own_cotan = jnp.where(flags[:, None], jnp.zeros_like(got_cotan), got_cotan)

    all_embeds = jnp.concatenate([got_embeds, hot_embeds], axis=0)
    all_cotan = jnp.concatenate([own_cotan, hot_cotan], axis=0)
    normed, hidden = trunk(all_embeds, trunk_gain, trunk_weight)
    active, d_gate, d_up, d_rows = through_expert(hidden, all_cotan, gate_w, up_w, down_w)

    share = feature // n
    block = padded(share, TILE // 2)
    column = jnp.arange(n * block, dtype=jnp.int32)
    source = jnp.where(column % block < share, column // block * share + column % block, -1)
    spread = (source[:, None] == jnp.arange(feature, dtype=jnp.int32)[None, :]).astype(
        jnp.bfloat16
    )
    normed_lines = dot_t(spread, normed).astype(jnp.bfloat16)
    grad_trunk = reduce_scatter(normed_lines, d_rows, block, n, experts_axis)[:share]

    grad_gate = t_dot(hidden, d_gate).astype(jnp.bfloat16)[None]
    grad_up = t_dot(hidden, d_up).astype(jnp.bfloat16)[None]
    grad_down = t_dot(active, all_cotan).astype(jnp.bfloat16)[None]
    return (grad_gate, grad_up, grad_down, grad_trunk)


def solution(mesh):
    spread_rows = P(("dp", "expert"), None)
    spread_first = P(("dp", "expert"), None, None)
    return jax.shard_map(
        body,
        mesh=mesh,
        in_specs=(
            spread_rows,
            P(),
            P(),
            spread_first,
            spread_first,
            spread_first,
            P(("dp", "expert")),
            P(),
            P(("dp", "expert")),
            spread_rows,
        ),
        out_specs=(spread_first, spread_first, spread_first, spread_rows),
        check_vma=False,
    )
```
